32 devices in a mesh: ctx: 8 (over y, x, core), head: 4 (over z).
Axes of the slice: x: 2, y: 2, z: 4, core: 2. Of those that a mesh axis runs over, the one named last changes fastest.
Arguments:
- queries: bfloat16 [2048, 4096], P('ctx', 'head'), may hold values from -168 to 168, as said below
- keys: bfloat16 [2048, 1024], P('ctx', 'head'), may hold values from -6.05 to 6.05, as said below
- values: bfloat16 [2048, 1024], P('ctx', 'head'), may hold values from -6 to 6
- d_y: bfloat16 [2048, 4096], P('ctx', 'head'), may hold values from -6 to 6
- w_out: bfloat16 [4096, 4096], P('head'), may hold values from -0.09375 to 0.09375
- key_blocks: int32 [16, 8], replicated, may hold values from 0 to 15, as said below
- block_count: int32 [16], replicated, may hold values from 1 to 8, as said below
Outputs:
- d_queries: bfloat16 [2048, 4096], P('ctx', 'head')
- keys_gradient: bfloat16 [2048, 1024], P('ctx', 'head')
- values_gradient: bfloat16 [2048, 1024], P('ctx', 'head')
The draws below stay inside these ranges and needn't reach their ends.
Inputs may be any that keep to these rules, and one draw needn't show every extreme that they name: `key_blocks`: each row holds 8 distinct block numbers; its first block_count entries are at most the query block's own number, and the first entry is that number. Later entries are read by nobody. `block_count`: the last query block has 8 live entries; query block b has at most b // 2 + 1. `queries`: values stay within the bound. `keys`: values stay within the bound.
All inputs are finite; a program needn't handle non-finite values.
Results may differ from the reference program's by a relative error of at most 0.017.
Values may be sent and summed in bfloat16 or wider, within the bound.
A program may use at most 64 MiB of HBM per device.

```python
import jax
import jax.numpy as jnp
from jax import lax

D = 4096
HQ = 32
SHARED_KV_SLOTS = 8
FEATURE_WIDTH = 128
QUERY_GROUP = 4
SPAN_LENGTH = 128
TOKEN_COUNT = 2048
QUERY_BLOCKS = 16
VISIBLE_SPANS = 8


def unshaped_keys(key):
    return jax.random.truncated_normal(jax.random.fold_in(key, 11), -6.0, 6.0, (TOKEN_COUNT, SHARED_KV_SLOTS * FEATURE_WIDTH), jnp.float32)


def draw_keys(key, part):
    base_offset = unshaped_keys(key)
    return base_offset.astype(jnp.bfloat16)


def draw_queries(key, part):
    base_offset = jax.random.truncated_normal(jax.random.fold_in(key, 12), -6.0, 6.0, (TOKEN_COUNT, HQ * FEATURE_WIDTH), jnp.float32)
    return base_offset.astype(jnp.bfloat16)


def mask_tables(key):
    block_indices = jnp.arange(QUERY_BLOCKS, dtype=jnp.int32)
    low = block_indices // 4
    high = block_indices // 2 + 1
    counts = jax.random.randint(jax.random.fold_in(key, 21), (QUERY_BLOCKS,), low, high) + 1
    counts = jnp.where(block_indices == QUERY_BLOCKS - 1, VISIBLE_SPANS, counts).astype(jnp.int32)
    starts = jax.random.randint(jax.random.fold_in(key, 22), (QUERY_BLOCKS,), 0, 4) == 0
    turn_ids = jnp.cumsum(starts.astype(jnp.int32))
    rows = block_indices[:, None]
    cols = block_indices[None, :]
    earlier = cols < rows
    same_turn = turn_ids[None, :] == turn_ids[:, None]
    priority = jnp.where(cols == rows, 4, jnp.where(earlier & (cols == 0), 3, jnp.where(earlier & same_turn, 2, jnp.where(earlier, 1, 0))))
    noise = jax.random.randint(jax.random.fold_in(key, 23), (QUERY_BLOCKS, QUERY_BLOCKS), 0, 4096)
    ranking = priority * 2 ** 24 + noise * QUERY_BLOCKS + cols
    _, chosen = jax.lax.top_k(ranking.astype(jnp.int32), VISIBLE_SPANS)
    return (chosen.astype(jnp.int32), counts)


def draw_key_blocks(key, part):
    return mask_tables(key)[0]


def draw_block_count(key, part):
    return mask_tables(key)[1]


def block_scale(own_key, shape, shards, low, largest):
    gain, own = 1.0, jax.random.fold_in(own_key, 6)
    for dim, parts in shards:
        draws = jnp.exp(jax.random.uniform(jax.random.fold_in(own, dim), (parts,), jnp.float32, low / len(shards), largest / len(shards)))
        gain = gain * jnp.repeat(draws, shape[dim] // parts).reshape([-1 if axis == dim else 1 for axis in range(len(shape))])
    return gain


def gaussian(key, dims, deviation, reach, pieces=(), held_as=jnp.bfloat16):
    drawn = deviation * jax.random.normal(key, dims, jnp.float32)
    if pieces:
        drawn = drawn * block_scale(key, dims, pieces, -0.22, 0.18)
    return jnp.clip(drawn, -reach, reach).astype(held_as)


def setup_inputs(seed: int = 0) -> dict:
    splits = jax.random.split(jax.random.key(seed), 8)
    return {
        "queries": draw_queries(jax.random.fold_in(splits[7], 71), 0),
        "keys": draw_keys(jax.random.fold_in(splits[7], 71), 0),
        "values": gaussian(splits[2], (TOKEN_COUNT, SHARED_KV_SLOTS * FEATURE_WIDTH), 1.0, 6.0, ((0, 8), (1, 4))),
        "d_y": gaussian(splits[3], (TOKEN_COUNT, D), 1.0, 6.0, ((0, 8), (1, 4))),
        "w_out": gaussian(splits[4], (HQ * FEATURE_WIDTH, D), (HQ * FEATURE_WIDTH) ** -0.5, 0.09375, ((0, 4),)),
        "key_blocks": draw_key_blocks(jax.random.fold_in(splits[7], 71), 0),
        "block_count": draw_block_count(jax.random.fold_in(splits[7], 71), 0),
    }


def block_grads(query_block_rows, gradient_rows, key_everything, value_everything, key_blocks, block_count, query_blk):
    score_scale = 1.0 / (FEATURE_WIDTH ** 0.5)
    block_indices = key_blocks[query_blk]
    key_selected = key_everything.reshape(QUERY_BLOCKS, SPAN_LENGTH, SHARED_KV_SLOTS, FEATURE_WIDTH)[block_indices].reshape(VISIBLE_SPANS * SPAN_LENGTH, SHARED_KV_SLOTS, FEATURE_WIDTH).astype(jnp.float32)
    value_selected = value_everything.reshape(QUERY_BLOCKS, SPAN_LENGTH, SHARED_KV_SLOTS, FEATURE_WIDTH)[block_indices].reshape(VISIBLE_SPANS * SPAN_LENGTH, SHARED_KV_SLOTS, FEATURE_WIDTH).astype(jnp.float32)
    asker_vectors_wide = query_block_rows.reshape(SPAN_LENGTH, SHARED_KV_SLOTS, QUERY_GROUP, FEATURE_WIDTH).astype(jnp.float32)
    upstream_derivative_wide = gradient_rows.reshape(SPAN_LENGTH, SHARED_KV_SLOTS, QUERY_GROUP, FEATURE_WIDTH).astype(jnp.float32)
    slot_live = jnp.arange(VISIBLE_SPANS, dtype=jnp.int32) < block_count[query_blk]
    key_pos = (block_indices[:, None] * SPAN_LENGTH + jnp.arange(SPAN_LENGTH, dtype=jnp.int32)[None, :]).reshape(VISIBLE_SPANS * SPAN_LENGTH)
    key_live = jnp.repeat(slot_live, SPAN_LENGTH)
    query_pos = query_blk * SPAN_LENGTH + jnp.arange(SPAN_LENGTH, dtype=jnp.int32)
    allowed = key_live[None, :] & (key_pos[None, :] <= query_pos[:, None])
    scores = jnp.einsum('ihgd,jhd->hgij', asker_vectors_wide, key_selected) * score_scale
    scores = jnp.where(allowed, scores, -jnp.inf)
    row_max = jnp.max(scores, axis=-1, keepdims=True)
    log_total = row_max + jnp.log(jnp.sum(jnp.exp(scores - row_max), axis=-1, keepdims=True))
    probs = jnp.where(allowed, jnp.exp(scores - log_total), 0.0)
    d_probs = jnp.einsum('ihgd,jhd->hgij', upstream_derivative_wide, value_selected)
    row_delta = jnp.sum(probs * d_probs, axis=-1, keepdims=True)
    logit_derivative = lax.optimization_barrier((probs * (d_probs - row_delta) * score_scale).astype(jnp.bfloat16)).astype(jnp.float32)
    attention_weights_narrow = lax.optimization_barrier(probs.astype(jnp.bfloat16)).astype(jnp.float32)
    d_query = jnp.einsum('hgij,jhd->ihgd', logit_derivative, key_selected).reshape(SPAN_LENGTH, HQ * FEATURE_WIDTH)
    lookup_derivative = jnp.einsum('ftbu,bfth->ufh', logit_derivative, asker_vectors_wide).reshape(VISIBLE_SPANS, SPAN_LENGTH, SHARED_KV_SLOTS * FEATURE_WIDTH)
    payload_derivative = jnp.einsum('ftbu,bfth->ufh', attention_weights_narrow, upstream_derivative_wide).reshape(VISIBLE_SPANS, SPAN_LENGTH, SHARED_KV_SLOTS * FEATURE_WIDTH)
    return d_query.astype(jnp.bfloat16), lookup_derivative, payload_derivative, block_indices


def reference(queries, keys, values, d_y, w_out, key_blocks, block_count):
    att_grad = jnp.dot(d_y, w_out.T, preferred_element_type=jnp.float32).astype(jnp.bfloat16)

    def step(carried, query_blk):
        key_gradient_total, value_gradient_total = carried
        query_block_rows = lax.dynamic_slice_in_dim(queries, query_blk * SPAN_LENGTH, SPAN_LENGTH, 0)
        gradient_rows = lax.dynamic_slice_in_dim(att_grad, query_blk * SPAN_LENGTH, SPAN_LENGTH, 0)
        d_query, lookup_derivative, payload_derivative, block_indices = block_grads(query_block_rows, gradient_rows, keys, values, key_blocks, block_count, query_blk)
        key_gradient_total = key_gradient_total.at[block_indices].add(lookup_derivative)
        value_gradient_total = value_gradient_total.at[block_indices].add(payload_derivative)
        return (key_gradient_total, value_gradient_total), d_query

    zeroed_totals = jnp.zeros((QUERY_BLOCKS, SPAN_LENGTH, SHARED_KV_SLOTS * FEATURE_WIDTH), jnp.float32)
    (key_gradient_total, value_gradient_total), d_queries = lax.scan(step, (zeroed_totals, zeroed_totals), jnp.arange(QUERY_BLOCKS, dtype=jnp.int32))
    d_queries = d_queries.reshape(TOKEN_COUNT, HQ * FEATURE_WIDTH)
    keys_gradient = key_gradient_total.reshape(TOKEN_COUNT, SHARED_KV_SLOTS * FEATURE_WIDTH).astype(jnp.bfloat16)
    values_gradient = value_gradient_total.reshape(TOKEN_COUNT, SHARED_KV_SLOTS * FEATURE_WIDTH).astype(jnp.bfloat16)
    return (d_queries, keys_gradient, values_gradient)
```

```python
import functools
import math

import jax
import jax.numpy as jnp
from jax import lax
from jax.experimental import pallas as pl
from jax.experimental.pallas import tpu as pltpu
from jax.sharding import PartitionSpec as P

FW = 128
SPAN = 128
PAIR = 2
MESH = pl.DeviceIdType.MESH
F32 = jnp.float32
BF16 = jnp.bfloat16


def dot(a, b, dims):
    return lax.dot_general(a, b, (dims, ((), ())), preferred_element_type=F32)


NN = ((1,), (0,))
NT = ((1,), (1,))
TN = ((0,), (0,))


def kernel(
    n_ctx, n_head, ob, slots, heads, group,
    kb_ref, cnt_ref, q_ref, k_ref, v_ref, dy_ref, w_ref,
    dq_ref, dk_ref, dv_ref,
    kv_own, kv_all, kv_loc, dy_all, w_buf, inv, qt, qn, gt, gn, gacc, ot, p_buf, dq_acc, part, own,
    w_sem, dn_send, up_send, dy_recv, kv_send, kvf_send, kv_recv, x_send_sem, x_recv_sem, s_send_sem, s_recv_sem, *exchange,
):
    scale = 1.0 / math.sqrt(FW)
    me = lax.axis_index("ctx")
    z = lax.axis_index("head")
    core = lax.rem(me, 2)
    chip = me // 2
    partner = me + 1 - 2 * core
    n_chip = n_ctx // 2
    kvw = heads * FW
    rows = group * SPAN
    xsend, xrecv, ssend, srecv = (exchange[e * heads : (e + 1) * heads] for e in range(4))

    barrier = pltpu.get_barrier_semaphore()

    @pl.loop(1, n_ctx)
    def _(step):
        pl.semaphore_signal(
            barrier, inc=1, device_id=(lax.rem(me + step, n_ctx), z), device_id_type=MESH
        )

    @pl.when(z > 0)
    def _():
        pl.semaphore_signal(barrier, inc=1, device_id=(me, z - 1), device_id_type=MESH)

    @pl.when(z < n_head - 1)
    def _():
        pl.semaphore_signal(barrier, inc=1, device_id=(me, z + 1), device_id_type=MESH)

    dh = dy_ref.shape[2]

    def w_copy(shard):
        return pltpu.make_async_copy(
            w_ref.at[:, pl.ds(pl.multiple_of(shard * dh, dh), dh)], w_buf.at[shard], w_sem.at[shard]
        )

    @pl.loop(0, n_head)
    def _(step):
        w_copy(lax.rem(z + step, n_head)).start()

    kv_own[:, :, 0:kvw] = k_ref[...]
    kv_own[:, :, kvw : 2 * kvw] = v_ref[...]

    ends = jnp.where(z > 0, 1, 0) + jnp.where(z < n_head - 1, 1, 0)
    pl.semaphore_wait(barrier, n_ctx - 1 + ends)

    def dy_copy(half, shard, src, down):
        sems = dn_send if down else up_send
        return pltpu.make_async_remote_copy(
            src_ref=src,
            dst_ref=dy_all.at[shard, half],
            send_sem=sems.at[half, shard],
            recv_sem=dy_recv.at[half, shard],
            device_id=(me, z - 1 if down else z + 1),
            device_id_type=MESH,
        )

    def send_own(half):
        @pl.when(z > 0)
        def _():
            dy_copy(half, z, dy_ref.at[half], True).start()

        @pl.when(z < n_head - 1)
        def _():
            dy_copy(half, z, dy_ref.at[half], False).start()

    def take(half, d):
        @pl.when(z + d < n_head)
        def _():
            copy = dy_copy(half, z + d, dy_all.at[z + d, half], True)
            copy.wait_recv()

            @pl.when(z > 0)
            def _():
                copy.start()

        @pl.when(z - d >= 0)
        def _():
            copy = dy_copy(half, z - d, dy_all.at[z - d, half], False)
            copy.wait_recv()

            @pl.when(z < n_head - 1)
            def _():
                copy.start()

    send_own(0)

    def kv_copy(owner, target, sem, src=None):
        return pltpu.make_async_remote_copy(
            src_ref=kv_all.at[owner] if src is None else src,
            dst_ref=kv_all.at[owner],
            send_sem=sem,
            recv_sem=kv_recv.at[owner],
            device_id=(target, z),
            device_id_type=MESH,
        )

    @pl.when(core == 0)
    def _():
        kv_copy(me, partner, kvf_send.at[chip], kv_own).start()

    @pl.loop(chip + 1, n_chip)
    def _(other):
        kv_copy(me, 2 * other + core, kv_send.at[other], kv_own).start()

    def table(i):
        blk = me * ob + i
        count = cnt_ref[blk]

        @pl.loop(0, (me + 1) * ob)
        def _(c):
            def look(s, found):
                hit = jnp.logical_and(kb_ref[blk, s] == c, s < count)
                return jnp.where(hit, s, found)

            inv[i, c] = lax.fori_loop(0, slots, look, jnp.int32(slots))

    for i in range(ob):
        for h in range(heads):
            u = i * heads + h
            part[u, slots] = jnp.zeros((SPAN, 2 * FW), F32)
            for g in range(group):
                col = (h * group + g) * FW
                tile = q_ref[i, :, col : col + FW]
                qn[u, g * SPAN : (g + 1) * SPAN, :] = tile
                qt[u, :, g * SPAN : (g + 1) * SPAN] = tile.astype(F32).T.astype(BF16)

    def project(half, shard, dy):
        if half == 0:
            w_copy(shard).wait()
        gacc[...] += dot(w_buf[shard], dy, NT)

    def project_at(half, d):
        @pl.when(z + d < n_head)
        def _():
            project(half, z + d, dy_all[z + d, half])

        @pl.when(z - d >= 0)
        def _():
            project(half, z - d, dy_all[z - d, half])

    def project_own(half):
        gacc[...] = jnp.zeros_like(gacc)
        project(half, z, dy_ref[half])

    def finish_projection(half):
        for h in range(heads):
            u = half * heads + h
            for g in range(group):
                row = (h * group + g) * FW
                tile = gacc[row : row + FW, :]
                gt[u, :, g * SPAN : (g + 1) * SPAN] = tile.astype(BF16)
                gn[u, g * SPAN : (g + 1) * SPAN, :] = tile.T.astype(BF16)

    def block_of(i, slot):
        blk = me * ob + i
        live = slot < cnt_ref[blk]
        c = jnp.where(live, kb_ref[blk, slot], blk)
        return c, jnp.where(live, (blk - c) * SPAN, -4 * SPAN)

    def rows_of(i, pair, col):
        return jnp.concatenate(
            [kv_loc[block_of(i, pair * PAIR + e)[0], :, col : col + FW] for e in range(PAIR)], axis=0
        )

    def pairs(i):
        return (jnp.minimum((me * ob + i) // 2 + 1, slots) + PAIR - 1) // PAIR

    def softmax(i, h):
        u = i * heads + h
        ahead = lax.broadcasted_iota(jnp.int32, (SPAN, rows), 0) - lax.rem(
            lax.broadcasted_iota(jnp.int32, (SPAN, rows), 1), SPAN
        )

        def scores(pair, top):
            s = dot(rows_of(i, pair, h * FW), qt[u], NN)
            masked = [
                jnp.where(ahead <= block_of(i, pair * PAIR + e)[1], s[e * SPAN : (e + 1) * SPAN], -1e30)
                for e in range(PAIR)
            ]
            s = jnp.concatenate(masked, axis=0)
            p_buf[u, pair] = s
            return jnp.maximum(top, jnp.max(s, axis=0, keepdims=True))

        top = lax.fori_loop(0, pairs(i), scores, jnp.full((1, rows), -1e30, F32))

        def exps(pair, total):
            e = jnp.exp((p_buf[u, pair] - top) * scale)
            p_buf[u, pair] = e
            return total + jnp.sum(e, axis=0, keepdims=True)

        total = lax.fori_loop(0, pairs(i), exps, jnp.zeros((1, rows), F32))
        part_of = 1.0 / total
        ot[u] = jnp.zeros((FW, rows), F32)

        @pl.loop(0, pairs(i))
        def _(pair):
            p = p_buf[u, pair] * part_of
            p_buf[u, pair] = p
            high = p.astype(BF16)
            low = (p - high.astype(F32)).astype(BF16)
            v = rows_of(i, pair, kvw + h * FW)
            ot[u] += dot(v, high, TN) + dot(v, low, TN)

    def gradients(i, h):
        u = i * heads + h
        delta = jnp.sum(gt[u].astype(F32) * ot[u], axis=0, keepdims=True)
        dq_acc[...] = jnp.zeros_like(dq_acc)

        @pl.loop(0, pairs(i))
        def _(pair):
            p = p_buf[u, pair]
            dp = dot(rows_of(i, pair, kvw + h * FW), gt[u], NN)
            ds = (p * (dp - delta)).astype(BF16)
            dk = dot(ds, qn[u], NN) * scale
            dv = dot(p.astype(BF16), gn[u], NN)
            both = jnp.concatenate([dk, dv], axis=1)
            for e in range(PAIR):
                part[u, pair * PAIR + e] = both[e * SPAN : (e + 1) * SPAN]
            dq_acc[...] += dot(rows_of(i, pair, h * FW), ds, TN)

        for g in range(group):
            col = (h * group + g) * FW
            dq_ref[i, :, col : col + FW] = (dq_acc[:, g * SPAN : (g + 1) * SPAN].T * scale).astype(BF16)

    def term(h, c):
        total = part[h, inv[0, c]]
        for i in range(1, ob):
            total = total + part[i * heads + h, inv[i, c]]
        return total

    def x_copy(h, other):
        return pltpu.make_async_remote_copy(
            src_ref=xsend[h].at[other],
            dst_ref=xrecv[h].at[other],
            send_sem=x_send_sem.at[h, other],
            recv_sem=x_recv_sem.at[h, other],
            device_id=(partner, z),
            device_id_type=MESH,
        )

    def s_copy(h, target, source):
        return pltpu.make_async_remote_copy(
            src_ref=ssend[h].at[target],
            dst_ref=srecv[h].at[source],
            send_sem=s_send_sem.at[h, target],
            recv_sem=s_recv_sem.at[h, source],
            device_id=(2 * target + core, z),
            device_id_type=MESH,
        )

    def for_chips(when, body):
        for other in range(n_chip):
            pl.when(when(other))(functools.partial(body, other))

    def swap_terms(h):
        def fill(other):
            for j in range(ob):
                xsend[h][other, j] = term(h, (2 * other + 1 - core) * ob + j).astype(BF16)

        for_chips(lambda other: other < chip + core, fill)
        for_chips(lambda other: other < chip + core, lambda other: x_copy(h, other).start())

    def send_terms(h):
        def fill(other):
            for j in range(ob):
                total = term(h, (2 * other + core) * ob + j) + xrecv[h][other, j].astype(F32)
                ssend[h][other, j] = total.astype(BF16)

        for_chips(lambda other: other < chip + 1 - core, lambda other: x_copy(h, other).wait_recv())
        for_chips(lambda other: other < chip, fill)
        for_chips(lambda other: other < chip, lambda other: s_copy(h, other, chip).start())

    def own_terms(h):
        for j in range(ob):
            own[h, j] = term(h, me * ob + j)

        def add(other):
            own[h] += xrecv[h][other].astype(F32)

        for_chips(lambda other: jnp.logical_and(other == chip, core == 0), add)

    def finish_terms(h):
        def add(source):
            own[h] += srecv[h][source].astype(F32)

        for_chips(lambda source: source > chip, lambda source: s_copy(h, chip, source).wait_recv())
        for_chips(lambda source: source > chip, add)

        dk_ref[:, :, h * FW : (h + 1) * FW] = own[h, :, :, 0:FW].astype(BF16)
        dv_ref[:, :, h * FW : (h + 1) * FW] = own[h, :, :, FW : 2 * FW].astype(BF16)

    project_own(0)
    for d in range(1, max(n_head - 1, 2)):
        take(0, d)
        if d == 1:
            @pl.loop(0, chip)
            def _(other):
                owner = 2 * other + core
                copy = kv_copy(owner, partner, kvf_send.at[other])
                copy.wait_recv()
                copy.start()

        if d == max(n_head - 2, 1):
            for i in range(1, ob):
                send_own(i)
        project_at(0, d)
    for i in range(ob):
        table(i)

    @pl.loop(0, chip + core)
    def _(other):
        kv_copy(2 * other + 1 - core, partner, kvf_send.at[0]).wait_recv()

    kv_loc[pl.ds(me * ob, ob)] = kv_own[...]

    @pl.loop(0, me)
    def _(owner):
        kv_loc[pl.ds(owner * ob, ob)] = kv_all[owner]

    for h in range(heads):
        softmax(0, h)
    for d in range(max(n_head - 1, 2), n_head):
        take(0, d)
        project_at(0, d)
    finish_projection(0)
    for i in range(1, ob):
        project_own(i)
        for d in range(1, n_head):
            take(i, d)
            if d == 1:
                for h in range(heads):
                    gradients(i - 1, h)
            if d == n_head - 2:
                for h in range(heads):
                    softmax(i, h)
            project_at(i, d)
        finish_projection(i)
    for h in range(heads):
        gradients(ob - 1, h)
        if h > 0:
            send_terms(h - 1)
        swap_terms(h)
    send_terms(heads - 1)
    for h in range(heads):
        own_terms(h)
    for h in range(heads):
        finish_terms(h)

    for half in range(ob):
        @pl.when(z > 0)
        def _(half=half):
            dy_copy(half, z, dy_ref.at[half], True).wait_send()

            @pl.loop(z + 1, n_head)
            def _(shard):
                dy_copy(half, shard, dy_all.at[shard, half], True).wait_send()

        @pl.when(z < n_head - 1)
        def _(half=half):
            dy_copy(half, z, dy_ref.at[half], False).wait_send()

            @pl.loop(0, z)
            def _(shard):
                dy_copy(half, shard, dy_all.at[shard, half], False).wait_send()

    @pl.when(core == 0)
    def _():
        kv_copy(me, partner, kvf_send.at[chip], kv_own).wait_send()

    @pl.loop(0, chip)
    def _(other):
        kv_copy(2 * other + core, partner, kvf_send.at[other]).wait_send()

    @pl.loop(chip + 1, n_chip)
    def _(other):
        kv_copy(me, 2 * other + core, kv_send.at[other], kv_own).wait_send()

    for h in range(heads):
        for_chips(lambda other: other < chip + core, lambda other: x_copy(h, other).wait_send())
        for_chips(lambda other: other < chip, lambda other: s_copy(h, other, chip).wait_send())


def per_device(n_ctx, n_head, queries, keys, values, d_y, w_out, key_blocks, block_count):
    tokens, qw = queries.shape
    kvw = keys.shape[1]
    dh = d_y.shape[1]
    ob = tokens // SPAN
    heads = kvw // FW
    group = qw // kvw
    slots = key_blocks.shape[1]
    n_chip = n_ctx // 2
    units = ob * heads
    rows = group * SPAN
    vmem = pl.BlockSpec(memory_space=pltpu.VMEM)
    smem = pl.BlockSpec(memory_space=pltpu.SMEM)
    dma = pltpu.SemaphoreType.DMA
    tiles = (n_chip, ob, SPAN, 2 * FW)

    def blocks(a):
        return a.reshape(ob, SPAN, a.shape[1])

    dq, dk, dv = pl.pallas_call(
        functools.partial(kernel, n_ctx, n_head, ob, slots, heads, group),
        out_shape=(
            jax.ShapeDtypeStruct((ob, SPAN, qw), BF16),
            jax.ShapeDtypeStruct((ob, SPAN, kvw), BF16),
            jax.ShapeDtypeStruct((ob, SPAN, kvw), BF16),
        ),
        in_specs=[smem, smem, vmem, vmem, vmem, vmem, pl.BlockSpec(memory_space=pl.ANY)],
        out_specs=(vmem, vmem, vmem),
        scratch_shapes=[
            pltpu.VMEM((ob, SPAN, 2 * kvw), BF16),
            pltpu.VMEM((n_ctx, ob, SPAN, 2 * kvw), BF16),
            pltpu.VMEM((n_ctx * ob, SPAN, 2 * kvw), BF16),
            pltpu.VMEM((n_head, ob, SPAN, dh), BF16),
            pltpu.VMEM((n_head, qw, dh), BF16),
            pltpu.SMEM((ob, n_ctx * ob), jnp.int32),
            pltpu.VMEM((units, FW, rows), BF16),
            pltpu.VMEM((units, rows, FW), BF16),
            pltpu.VMEM((units, FW, rows), BF16),
            pltpu.VMEM((units, rows, FW), BF16),
            pltpu.VMEM((qw, SPAN), F32),
            pltpu.VMEM((units, FW, rows), F32),
            pltpu.VMEM((units, -(-slots // PAIR), PAIR * SPAN, rows), F32),
            pltpu.VMEM((FW, rows), F32),
            pltpu.VMEM((units, slots + 1, SPAN, 2 * FW), F32),
            pltpu.VMEM((heads, ob, SPAN, 2 * FW), F32),
            dma((n_head,)),
            dma((ob, n_head)),
            dma((ob, n_head)),
            dma((ob, n_head)),
            dma((n_chip,)),
            dma((n_chip,)),
            dma((n_ctx,)),
            dma((heads, n_chip)),
            dma((heads, n_chip)),
            dma((heads, n_chip)),
            dma((heads, n_chip)),
            *[pltpu.VMEM(tiles, BF16) for _ in range(4 * heads)],
        ],
        compiler_params=pltpu.CompilerParams(
            collective_id=0, has_side_effects=True, vmem_limit_bytes=60 * 1024 * 1024
        ),
        cost_estimate=pl.CostEstimate(
            flops=2 * tokens * dh * n_head * qw, bytes_accessed=2 * w_out.size, transcendentals=0
        ),
    )(key_blocks, block_count, blocks(queries), blocks(keys), blocks(values), blocks(d_y), w_out)
    return dq.reshape(tokens, qw), dk.reshape(tokens, kvw), dv.reshape(tokens, kvw)


def solution(mesh):
    sharded = P("ctx", "head")
    return jax.shard_map(
        functools.partial(per_device, mesh.shape["ctx"], mesh.shape["head"]),
        mesh=mesh,
        in_specs=(sharded, sharded, sharded, sharded, P("head", None), P(), P()),
        out_specs=(sharded, sharded, sharded),
        check_vma=False,
    )
```

```python
import functools
import math

import jax
import jax.numpy as jnp
from jax import lax
from jax.experimental import pallas as pl
from jax.experimental.pallas import tpu as pltpu
from jax.sharding import PartitionSpec as P

FW = 128
SPAN = 128
PAIR = 2
MESH = pl.DeviceIdType.MESH
F32 = jnp.float32
BF16 = jnp.bfloat16


def dot(a, b, dims):
    return lax.dot_general(a, b, (dims, ((), ())), preferred_element_type=F32)


NN = ((1,), (0,))
NT = ((1,), (1,))
TN = ((0,), (0,))


def kernel(
    n_ctx, n_head, ob, slots, heads, group,
    kb_hbm, cnt_ref, q_hbm, k_hbm, v_hbm, dy_ref, w_ref,
    dq_ref, dk_ref, dv_ref,
    kb_ref, q_ref, in_sem,
    kv_own, kv_all, kv_loc, dy_all, w_buf, inv, qt, qn, gt, gn, gacc, ot, p_buf, dq_acc, part, own,
    w_sem, dn_send, up_send, dy_recv, kv_send, kvf_send, kv_recv, x_send_sem, x_recv_sem, s_send_sem, s_recv_sem, *exchange,
):
    scale = 1.0 / math.sqrt(FW)
    me = lax.axis_index("ctx")
    z = lax.axis_index("head")
    core = lax.rem(me, 2)
    chip = me // 2
    partner = me + 1 - 2 * core
    n_chip = n_ctx // 2
    kvw = heads * FW
    rows = group * SPAN
    xsend, xrecv, ssend, srecv = (exchange[e * heads : (e + 1) * heads] for e in range(4))

    barrier = pltpu.get_barrier_semaphore()

    @pl.loop(1, n_ctx)
    def _(step):
        pl.semaphore_signal(
            barrier, inc=1, device_id=(lax.rem(me + step, n_ctx), z), device_id_type=MESH
        )

    @pl.when(z > 0)
    def _():
        pl.semaphore_signal(barrier, inc=1, device_id=(me, z - 1), device_id_type=MESH)

    @pl.when(z < n_head - 1)
    def _():
        pl.semaphore_signal(barrier, inc=1, device_id=(me, z + 1), device_id_type=MESH)

    dh = dy_ref.shape[2]

    def w_copy(shard):
        return pltpu.make_async_copy(
            w_ref.at[:, pl.ds(pl.multiple_of(shard * dh, dh), dh)], w_buf.at[shard], w_sem.at[shard]
        )

    inputs = [
        pltpu.make_async_copy(src, dst, in_sem.at[e])
        for e, (src, dst) in enumerate(
            [
                (k_hbm, kv_own.at[:, :, 0:kvw]),
                (v_hbm, kv_own.at[:, :, kvw : 2 * kvw]),
                (dy_ref, dy_all.at[z]),
                (q_hbm, q_ref),
                (kb_hbm, kb_ref),
            ]
        )
    ]
    for copy in inputs:
        copy.start()

    @pl.loop(0, n_head)
    def _(step):
        w_copy(lax.rem(z + step, n_head)).start()

    ends = jnp.where(z > 0, 1, 0) + jnp.where(z < n_head - 1, 1, 0)
    pl.semaphore_wait(barrier, n_ctx - 1 + ends)

    def dy_copy(half, shard, src, down):
        sems = dn_send if down else up_send
        return pltpu.make_async_remote_copy(
            src_ref=src,
            dst_ref=dy_all.at[shard, half],
            send_sem=sems.at[half, shard],
            recv_sem=dy_recv.at[half, shard],
            device_id=(me, z - 1 if down else z + 1),
            device_id_type=MESH,
        )

    def send_own(half):
        @pl.when(z > 0)
        def _():
            dy_copy(half, z, dy_ref.at[half], True).start()

        @pl.when(z < n_head - 1)
        def _():
            dy_copy(half, z, dy_ref.at[half], False).start()

    inner = jnp.logical_and(z > 0, z < n_head - 1)
    outer = jnp.logical_not(inner)

    def hand_on(half, d):
        @pl.when(jnp.logical_and(inner, z + d < n_head))
        def _():
            copy = dy_copy(half, z + d, dy_all.at[z + d, half], True)
            copy.wait_recv()
            copy.start()

        @pl.when(jnp.logical_and(inner, z - d >= 0))
        def _():
            copy = dy_copy(half, z - d, dy_all.at[z - d, half], False)
            copy.wait_recv()
            copy.start()

    def take(half, d):
        @pl.when(jnp.logical_and(outer, z + d < n_head))
        def _():
            dy_copy(half, z + d, dy_all.at[z + d, half], True).wait_recv()

        @pl.when(jnp.logical_and(outer, z - d >= 0))
        def _():
            dy_copy(half, z - d, dy_all.at[z - d, half], False).wait_recv()

    send_own(0)
    inputs[0].wait()
    inputs[1].wait()

    def kv_copy(owner, target, sem, src=None):
        return pltpu.make_async_remote_copy(
            src_ref=kv_all.at[owner] if src is None else src,
            dst_ref=kv_all.at[owner],
            send_sem=sem,
            recv_sem=kv_recv.at[owner],
            device_id=(target, z),
            device_id_type=MESH,
        )

    @pl.when(core == 0)
    def _():
        kv_copy(me, partner, kvf_send.at[chip], kv_own).start()

    @pl.loop(chip + 1, n_chip)
    def _(other):
        kv_copy(me, 2 * other + core, kv_send.at[other], kv_own).start()

    def table(i):
        blk = me * ob + i
        count = cnt_ref[blk]

        @pl.loop(0, (me + 1) * ob)
        def _(c):
            def look(s, found):
                hit = jnp.logical_and(kb_ref[s, blk] == c, s < count)
                return jnp.where(hit, s, found)

            inv[i, c] = lax.fori_loop(0, slots, look, jnp.int32(slots))

    inputs[3].wait()
    for i in range(ob):
        for h in range(heads):
            u = i * heads + h
            part[u, slots] = jnp.zeros((SPAN, 2 * FW), F32)
            for g in range(group):
                col = (h * group + g) * FW
                tile = q_ref[i, :, col : col + FW]
                qn[u, g * SPAN : (g + 1) * SPAN, :] = tile
                qt[u, :, g * SPAN : (g + 1) * SPAN] = tile.astype(F32).T.astype(BF16)

    def project(half, shard, dy):
        if half == 0:
            w_copy(shard).wait()
        gacc[...] += dot(w_buf[shard], dy, NT)

    def project_at(half, d):
        @pl.when(z + d < n_head)
        def _():
            project(half, z + d, dy_all[z + d, half])

        @pl.when(z - d >= 0)
        def _():
            project(half, z - d, dy_all[z - d, half])

    def project_own(half):
        gacc[...] = jnp.zeros_like(gacc)
        project(half, z, dy_all[z, half])

    def finish_projection(half):
        for h in range(heads):
            u = half * heads + h
            for g in range(group):
                row = (h * group + g) * FW
                tile = gacc[row : row + FW, :]
                gt[u, :, g * SPAN : (g + 1) * SPAN] = tile.astype(BF16)
                gn[u, g * SPAN : (g + 1) * SPAN, :] = tile.T.astype(BF16)

    def block_of(i, slot):
        blk = me * ob + i
        live = slot < cnt_ref[blk]
        c = jnp.where(live, kb_ref[slot, blk], blk)
        return c, jnp.where(live, (blk - c) * SPAN, -4 * SPAN)

    def rows_of(i, pair, col):
        return jnp.concatenate(
            [kv_loc[block_of(i, pair * PAIR + e)[0], :, col : col + FW] for e in range(PAIR)], axis=0
        )

    def pairs(i):
        return (jnp.minimum((me * ob + i) // 2 + 1, slots) + PAIR - 1) // PAIR

    def softmax(i, h):
        u = i * heads + h
        ahead = lax.broadcasted_iota(jnp.int32, (SPAN, rows), 0) - lax.rem(
            lax.broadcasted_iota(jnp.int32, (SPAN, rows), 1), SPAN
        )

        def scores(pair, top):
            s = dot(rows_of(i, pair, h * FW), qt[u], NN)
            masked = [
                jnp.where(ahead <= block_of(i, pair * PAIR + e)[1], s[e * SPAN : (e + 1) * SPAN], -1e30)
                for e in range(PAIR)
            ]
            s = jnp.concatenate(masked, axis=0)
            p_buf[u, pair] = s
            return jnp.maximum(top, jnp.max(s, axis=0, keepdims=True))

        top = lax.fori_loop(0, pairs(i), scores, jnp.full((1, rows), -1e30, F32))

        def exps(pair, total):
            e = jnp.exp((p_buf[u, pair] - top) * scale)
            p_buf[u, pair] = e
            return total + jnp.sum(e, axis=0, keepdims=True)

        total = lax.fori_loop(0, pairs(i), exps, jnp.zeros((1, rows), F32))
        part_of = 1.0 / total
        ot[u] = jnp.zeros((FW, rows), F32)

        @pl.loop(0, pairs(i))
        def _(pair):
            p = p_buf[u, pair] * part_of
            p_buf[u, pair] = p
            high = p.astype(BF16)
            low = (p - high.astype(F32)).astype(BF16)
            v = rows_of(i, pair, kvw + h * FW)
            ot[u] += dot(v, high, TN) + dot(v, low, TN)

    def gradients(i, h):
        u = i * heads + h
        delta = jnp.sum(gt[u].astype(F32) * ot[u], axis=0, keepdims=True)
        dq_acc[...] = jnp.zeros_like(dq_acc)

        @pl.loop(0, pairs(i))
        def _(pair):
            p = p_buf[u, pair]
            dp = dot(rows_of(i, pair, kvw + h * FW), gt[u], NN)
            ds = (p * (dp - delta)).astype(BF16)
            dk = dot(ds, qn[u], NN) * scale
            dv = dot(p.astype(BF16), gn[u], NN)
            both = jnp.concatenate([dk, dv], axis=1)
            for e in range(PAIR):
                part[u, pair * PAIR + e] = both[e * SPAN : (e + 1) * SPAN]
            dq_acc[...] += dot(rows_of(i, pair, h * FW), ds, TN)

        for g in range(group):
            col = (h * group + g) * FW
            dq_ref[i, :, col : col + FW] = (dq_acc[:, g * SPAN : (g + 1) * SPAN].T * scale).astype(BF16)

    def term(h, c):
        total = part[h, inv[0, c]]
        for i in range(1, ob):
            total = total + part[i * heads + h, inv[i, c]]
        return total

    def x_copy(h, other):
        return pltpu.make_async_remote_copy(
            src_ref=xsend[h].at[other],
            dst_ref=xrecv[h].at[other],
            send_sem=x_send_sem.at[h, other],
            recv_sem=x_recv_sem.at[h, other],
            device_id=(partner, z),
            device_id_type=MESH,
        )

    def s_copy(h, target, source):
        return pltpu.make_async_remote_copy(
            src_ref=ssend[h].at[target],
            dst_ref=srecv[h].at[source],
            send_sem=s_send_sem.at[h, target],
            recv_sem=s_recv_sem.at[h, source],
            device_id=(2 * target + core, z),
            device_id_type=MESH,
        )

    def for_chips(when, body):
        for other in range(n_chip):
            pl.when(when(other))(functools.partial(body, other))

    def swap_terms(h):
        def fill(other):
            for j in range(ob):
                xsend[h][other, j] = term(h, (2 * other + 1 - core) * ob + j).astype(BF16)

        for_chips(lambda other: other < chip + core, fill)
        for_chips(lambda other: other < chip + core, lambda other: x_copy(h, other).start())

    def send_terms(h):
        def fill(other):
            for j in range(ob):
                total = term(h, (2 * other + core) * ob + j) + xrecv[h][other, j].astype(F32)
                ssend[h][other, j] = total.astype(BF16)

        for_chips(lambda other: other < chip + 1 - core, lambda other: x_copy(h, other).wait_recv())
        for_chips(lambda other: other < chip, fill)
        for_chips(lambda other: other < chip, lambda other: s_copy(h, other, chip).start())

    def own_terms(h):
        for j in range(ob):
            own[h, j] = term(h, me * ob + j)

    def finish_terms(h):
        def add(source):
            own[h] += srecv[h][source].astype(F32)

        for_chips(lambda source: source > chip, lambda source: s_copy(h, chip, source).wait_recv())
        for_chips(lambda source: source > chip, add)

        def add_partner(other):
            own[h] += xrecv[h][other].astype(F32)

        for_chips(lambda other: jnp.logical_and(other == chip, core == 0), add_partner)

        dk_ref[:, :, h * FW : (h + 1) * FW] = own[h, :, :, 0:FW].astype(BF16)
        dv_ref[:, :, h * FW : (h + 1) * FW] = own[h, :, :, FW : 2 * FW].astype(BF16)

    inputs[2].wait()
    project_own(0)
    for d in range(1, n_head - 1):
        hand_on(0, d)
        if d == 1:
            take(0, 1)
            for i in range(1, ob):
                pl.when(outer)(functools.partial(send_own, i))

            @pl.loop(0, chip)
            def _(other):
                copy = kv_copy(2 * other + core, partner, kvf_send.at[other])
                copy.wait_recv()
                copy.start()

            project_at(0, 1)
    for i in range(1, ob):
        pl.when(inner)(functools.partial(send_own, i))
    inputs[4].wait()
    for i in range(ob):
        table(i)

    @pl.loop(0, chip + core)
    def _(other):
        kv_copy(2 * other + 1 - core, partner, kvf_send.at[0]).wait_recv()

    kv_loc[pl.ds(me * ob, ob)] = kv_own[...]

    @pl.loop(0, me)
    def _(owner):
        kv_loc[pl.ds(owner * ob, ob)] = kv_all[owner]

    for h in range(heads):
        softmax(0, h)
    for i in range(1, ob):
        hand_on(i, 1)
        softmax(i, 0)
        for d in range(2, n_head - 1):
            hand_on(i, d)
        for h in range(1, heads):
            softmax(i, h)
    for d in range(2, n_head):
        take(0, d)
        project_at(0, d)
    finish_projection(0)
    for i in range(1, ob):
        for h in range(heads):
            gradients(i - 1, h)
        project_own(i)
        for d in range(1, n_head):
            take(i, d)
            project_at(i, d)
        finish_projection(i)
    for h in range(heads):
        gradients(ob - 1, h)
        swap_terms(h)
        own_terms(h)
        send_terms(h)
    for h in range(heads):
        finish_terms(h)

    for half in range(ob):
        @pl.when(z > 0)
        def _(half=half):
            dy_copy(half, z, dy_ref.at[half], True).wait_send()

            @pl.loop(z + 1, n_head)
            def _(shard):
                dy_copy(half, shard, dy_all.at[shard, half], True).wait_send()

        @pl.when(z < n_head - 1)
        def _(half=half):
            dy_copy(half, z, dy_ref.at[half], False).wait_send()

            @pl.loop(0, z)
            def _(shard):
                dy_copy(half, shard, dy_all.at[shard, half], False).wait_send()

    @pl.when(core == 0)
    def _():
        kv_copy(me, partner, kvf_send.at[chip], kv_own).wait_send()

    @pl.loop(0, chip)
    def _(other):
        kv_copy(2 * other + core, partner, kvf_send.at[other]).wait_send()

    @pl.loop(chip + 1, n_chip)
    def _(other):
        kv_copy(me, 2 * other + core, kv_send.at[other], kv_own).wait_send()

    for h in range(heads):
        for_chips(lambda other: other < chip + core, lambda other: x_copy(h, other).wait_send())
        for_chips(lambda other: other < chip, lambda other: s_copy(h, other, chip).wait_send())


def hand_out(dq, dk, dv, dq_out, dk_out, dv_out, sem):
    copies = [
        pltpu.make_async_copy(src, dst, sem.at[e])
        for e, (src, dst) in enumerate([(dq, dq_out), (dk, dk_out), (dv, dv_out)])
    ]
    for copy in copies:
        copy.start()
    for copy in copies:
        copy.wait()


def per_device(n_ctx, n_head, queries, keys, values, d_y, w_out, key_blocks, block_count):
    tokens, qw = queries.shape
    kvw = keys.shape[1]
    dh = d_y.shape[1]
    ob = tokens // SPAN
    heads = kvw // FW
    group = qw // kvw
    slots = key_blocks.shape[1]
    n_chip = n_ctx // 2
    units = ob * heads
    rows = group * SPAN
    vmem = pl.BlockSpec(memory_space=pltpu.VMEM)
    anywhere = pl.BlockSpec(memory_space=pl.ANY)
    smem = pl.BlockSpec(memory_space=pltpu.SMEM)
    dma = pltpu.SemaphoreType.DMA
    tiles = (n_chip, ob, SPAN, 2 * FW)

    def blocks(a):
        return a.reshape(ob, SPAN, a.shape[1])

    dq, dk, dv = pl.pallas_call(
        functools.partial(kernel, n_ctx, n_head, ob, slots, heads, group),
        out_shape=(
            jax.ShapeDtypeStruct((ob, SPAN, qw), BF16),
            jax.ShapeDtypeStruct((ob, SPAN, kvw), BF16),
            jax.ShapeDtypeStruct((ob, SPAN, kvw), BF16),
        ),
        in_specs=[anywhere, smem, anywhere, anywhere, anywhere, anywhere, anywhere],
        out_specs=(vmem, vmem, vmem),
        scratch_shapes=[
            pltpu.SMEM(key_blocks.shape[::-1], jnp.int32),
            pltpu.VMEM((ob, SPAN, qw), BF16),
            dma((5,)),
            pltpu.VMEM((ob, SPAN, 2 * kvw), BF16),
            pltpu.VMEM((n_ctx, ob, SPAN, 2 * kvw), BF16),
            pltpu.VMEM((n_ctx * ob, SPAN, 2 * kvw), BF16),
            pltpu.VMEM((n_head, ob, SPAN, dh), BF16),
            pltpu.VMEM((n_head, qw, dh), BF16),
            pltpu.SMEM((ob, n_ctx * ob), jnp.int32),
            pltpu.VMEM((units, FW, rows), BF16),
            pltpu.VMEM((units, rows, FW), BF16),
            pltpu.VMEM((units, FW, rows), BF16),
            pltpu.VMEM((units, rows, FW), BF16),
            pltpu.VMEM((qw, SPAN), F32),
            pltpu.VMEM((units, FW, rows), F32),
            pltpu.VMEM((units, -(-slots // PAIR), PAIR * SPAN, rows), F32),
            pltpu.VMEM((FW, rows), F32),
            pltpu.VMEM((units, slots + 1, SPAN, 2 * FW), F32),
            pltpu.VMEM((heads, ob, SPAN, 2 * FW), F32),
            dma((n_head,)),
            dma((ob, n_head)),
            dma((ob, n_head)),
            dma((ob, n_head)),
            dma((n_chip,)),
            dma((n_chip,)),
            dma((n_ctx,)),
            dma((heads, n_chip)),
            dma((heads, n_chip)),
            dma((heads, n_chip)),
            dma((heads, n_chip)),
            *[pltpu.VMEM(tiles, BF16) for _ in range(4 * heads)],
        ],
        compiler_params=pltpu.CompilerParams(
            collective_id=0, has_side_effects=True, vmem_limit_bytes=60 * 1024 * 1024
        ),
        cost_estimate=pl.CostEstimate(
            flops=2 * tokens * dh * n_head * qw, bytes_accessed=2 * w_out.size, transcendentals=0
        ),
    )(key_blocks.T, block_count, blocks(queries), blocks(keys), blocks(values), blocks(d_y), w_out)
    dq, dk, dv = pl.pallas_call(
        hand_out,
        out_shape=tuple(jax.ShapeDtypeStruct(a.shape, a.dtype) for a in (dq, dk, dv)),
        in_specs=[anywhere] * 3,
        out_specs=(anywhere,) * 3,
        scratch_shapes=[dma((3,))],
        compiler_params=pltpu.CompilerParams(vmem_limit_bytes=60 * 1024 * 1024),
    )(dq, dk, dv)
    return dq.reshape(tokens, qw), dk.reshape(tokens, kvw), dv.reshape(tokens, kvw)


def solution(mesh):
    sharded = P("ctx", "head")
    return jax.shard_map(
        functools.partial(per_device, mesh.shape["ctx"], mesh.shape["head"]),
        mesh=mesh,
        in_specs=(sharded, sharded, sharded, sharded, P("head", None), P(), P()),
        out_specs=(sharded, sharded, sharded),
        check_vma=False,
    )
```

```python
import functools
import math

import jax
import jax.numpy as jnp
from jax import lax
from jax.experimental import pallas as pl
from jax.experimental.pallas import tpu as pltpu
from jax.sharding import PartitionSpec as P

FW = 128
SPAN = 128
PAIR = 2
MESH = pl.DeviceIdType.MESH
F32 = jnp.float32
BF16 = jnp.bfloat16


def dot(a, b, dims):
    return lax.dot_general(a, b, (dims, ((), ())), preferred_element_type=F32)


NN = ((1,), (0,))
NT = ((1,), (1,))
TN = ((0,), (0,))


def kernel(
    n_ctx, n_head, ob, slots, heads, group,
    kb_hbm, cnt_ref, q_hbm, k_hbm, v_hbm, dy_ref, w_ref,
    dq_ref, dk_ref, dv_ref,
    kb_ref, q_ref, in_sem,
    kv_own, kv_all, kv_loc, dy_all, w_buf, inv, qt, qn, gt, gn, gacc, ot, p_buf, dq_acc, part, own, share, ds_buf,
    w_sem, dn_send, up_send, dy_recv, kv_send, kvf_send, kv_recv, x_send_sem, x_recv_sem, s_send_sem, s_recv_sem, *exchange,
):
    scale = 1.0 / math.sqrt(FW)
    me = lax.axis_index("ctx")
    z = lax.axis_index("head")
    core = lax.rem(me, 2)
    chip = me // 2
    partner = me + 1 - 2 * core
    n_chip = n_ctx // 2
    kvw = heads * FW
    rows = group * SPAN
    xsend, xrecv, ssend, srecv = (exchange[e * heads : (e + 1) * heads] for e in range(4))

    barrier = pltpu.get_barrier_semaphore()

    @pl.loop(1, n_ctx)
    def _(step):
        pl.semaphore_signal(
            barrier, inc=1, device_id=(lax.rem(me + step, n_ctx), z), device_id_type=MESH
        )

    @pl.when(z > 0)
    def _():
        pl.semaphore_signal(barrier, inc=1, device_id=(me, z - 1), device_id_type=MESH)

    @pl.when(z < n_head - 1)
    def _():
        pl.semaphore_signal(barrier, inc=1, device_id=(me, z + 1), device_id_type=MESH)

    dh = dy_ref.shape[2]

    def w_copy(shard):
        return pltpu.make_async_copy(
            w_ref.at[:, pl.ds(pl.multiple_of(shard * dh, dh), dh)], w_buf.at[shard], w_sem.at[shard]
        )

    inputs = [
        pltpu.make_async_copy(src, dst, in_sem.at[e])
        for e, (src, dst) in enumerate(
            [
                (k_hbm, kv_own.at[:, :, 0:kvw]),
                (v_hbm, kv_own.at[:, :, kvw : 2 * kvw]),
                (dy_ref, dy_all.at[z]),
                (q_hbm, q_ref),
                (kb_hbm, kb_ref),
            ]
        )
    ]
    for copy in inputs:
        copy.start()

    @pl.loop(0, n_head)
    def _(step):
        w_copy(lax.rem(z + step, n_head)).start()

    ends = jnp.where(z > 0, 1, 0) + jnp.where(z < n_head - 1, 1, 0)
    pl.semaphore_wait(barrier, n_ctx - 1 + ends)

    def dy_copy(half, shard, src, down):
        sems = dn_send if down else up_send
        return pltpu.make_async_remote_copy(
            src_ref=src,
            dst_ref=dy_all.at[shard, half],
            send_sem=sems.at[half, shard],
            recv_sem=dy_recv.at[half, shard],
            device_id=(me, z - 1 if down else z + 1),
            device_id_type=MESH,
        )

    def send_own(half):
        @pl.when(z > 0)
        def _():
            dy_copy(half, z, dy_ref.at[half], True).start()

        @pl.when(z < n_head - 1)
        def _():
            dy_copy(half, z, dy_ref.at[half], False).start()

    inner = jnp.logical_and(z > 0, z < n_head - 1)
    outer = jnp.logical_not(inner)

    def hand_on(half, d):
        @pl.when(jnp.logical_and(inner, z + d < n_head))
        def _():
            copy = dy_copy(half, z + d, dy_all.at[z + d, half], True)
            copy.wait_recv()
            copy.start()

        @pl.when(jnp.logical_and(inner, z - d >= 0))
        def _():
            copy = dy_copy(half, z - d, dy_all.at[z - d, half], False)
            copy.wait_recv()
            copy.start()

    def take(half, d):
        @pl.when(jnp.logical_and(outer, z + d < n_head))
        def _():
            dy_copy(half, z + d, dy_all.at[z + d, half], True).wait_recv()

        @pl.when(jnp.logical_and(outer, z - d >= 0))
        def _():
            dy_copy(half, z - d, dy_all.at[z - d, half], False).wait_recv()

    send_own(0)
    inputs[0].wait()
    inputs[1].wait()

    def kv_copy(owner, target, sem, src=None):
        return pltpu.make_async_remote_copy(
            src_ref=kv_all.at[owner] if src is None else src,
            dst_ref=kv_all.at[owner],
            send_sem=sem,
            recv_sem=kv_recv.at[owner],
            device_id=(target, z),
            device_id_type=MESH,
        )

    @pl.when(core == 0)
    def _():
        kv_copy(me, partner, kvf_send.at[chip], kv_own).start()

    @pl.loop(chip + 1, n_chip)
    def _(other):
        kv_copy(me, 2 * other + core, kv_send.at[other], kv_own).start()

    def table(i):
        blk = me * ob + i
        count = cnt_ref[blk]

        @pl.loop(0, (me + 1) * ob)
        def _(c):
            def look(s, found):
                hit = jnp.logical_and(kb_ref[s, blk] == c, s < count)
                return jnp.where(hit, s, found)

            inv[i, c] = lax.fori_loop(0, slots, look, jnp.int32(slots))

    inputs[3].wait()
    for i in range(ob):
        for h in range(heads):
            u = i * heads + h
            part[u, slots] = jnp.zeros((SPAN, 2 * FW), F32)
            for g in range(group):
                col = (h * group + g) * FW
                tile = q_ref[i, :, col : col + FW]
                qn[u, g * SPAN : (g + 1) * SPAN, :] = tile
                qt[u, :, g * SPAN : (g + 1) * SPAN] = tile.astype(F32).T.astype(BF16)

    def project(half, shard, dy):
        if half == 0:
            w_copy(shard).wait()
        gacc[...] += dot(w_buf[shard], dy, NT)

    def project_at(half, d):
        @pl.when(z + d < n_head)
        def _():
            project(half, z + d, dy_all[z + d, half])

        @pl.when(z - d >= 0)
        def _():
            project(half, z - d, dy_all[z - d, half])

    def project_own(half):
        gacc[...] = jnp.zeros_like(gacc)
        project(half, z, dy_all[z, half])

    def finish_projection(half):
        for h in range(heads):
            u = half * heads + h
            for g in range(group):
                row = (h * group + g) * FW
                tile = gacc[row : row + FW, :]
                gt[u, :, g * SPAN : (g + 1) * SPAN] = tile.astype(BF16)
                gn[u, g * SPAN : (g + 1) * SPAN, :] = tile.T.astype(BF16)

    def block_of(i, slot):
        blk = me * ob + i
        live = slot < cnt_ref[blk]
        c = jnp.where(live, kb_ref[slot, blk], blk)
        return c, jnp.where(live, (blk - c) * SPAN, -4 * SPAN)

    def rows_of(i, pair, col):
        return jnp.concatenate(
            [kv_loc[block_of(i, pair * PAIR + e)[0], :, col : col + FW] for e in range(PAIR)], axis=0
        )

    def pairs(i):
        return (jnp.minimum((me * ob + i) // 2 + 1, slots) + PAIR - 1) // PAIR

    def softmax(i, h):
        u = i * heads + h
        ahead = lax.broadcasted_iota(jnp.int32, (SPAN, rows), 0) - lax.rem(
            lax.broadcasted_iota(jnp.int32, (SPAN, rows), 1), SPAN
        )

        def scores(pair, top):
            s = dot(rows_of(i, pair, h * FW), qt[u], NN)
            masked = [
                jnp.where(ahead <= block_of(i, pair * PAIR + e)[1], s[e * SPAN : (e + 1) * SPAN], -1e30)
                for e in range(PAIR)
            ]
            s = jnp.concatenate(masked, axis=0)
            p_buf[u, pair] = s
            return jnp.maximum(top, jnp.max(s, axis=0, keepdims=True))

        top = lax.fori_loop(0, pairs(i), scores, jnp.full((1, rows), -1e30, F32))

        ot[u] = jnp.zeros((FW, rows), F32)

        def exps(pair, total):
            e = jnp.exp((p_buf[u, pair] - top) * scale)
            p_buf[u, pair] = e
            high = e.astype(BF16)
            low = (e - high.astype(F32)).astype(BF16)
            v = rows_of(i, pair, kvw + h * FW)
            ot[u] += dot(v, high, TN) + dot(v, low, TN)
            return total + jnp.sum(e, axis=0, keepdims=True)

        total = lax.fori_loop(0, pairs(i), exps, jnp.zeros((1, rows), F32))
        share[u] = 1.0 / total

    def gradients(i, h):
        u = i * heads + h
        part_of = share[u]
        delta = jnp.sum(gt[u].astype(F32) * ot[u], axis=0, keepdims=True) * part_of

        @pl.loop(0, pairs(i))
        def _(pair):
            p = p_buf[u, pair] * part_of
            dp = dot(rows_of(i, pair, kvw + h * FW), gt[u], NN)
            ds = (p * (dp - delta)).astype(BF16)
            dk = dot(ds, qn[u], NN) * scale
            dv = dot(p.astype(BF16), gn[u], NN)
            both = jnp.concatenate([dk, dv], axis=1)
            for e in range(PAIR):
                part[u, pair * PAIR + e] = both[e * SPAN : (e + 1) * SPAN]
            ds_buf[h, pair] = ds

    def query_gradient(i, h):
        dq_acc[...] = jnp.zeros_like(dq_acc)

        @pl.loop(0, pairs(i))
        def _(pair):
            dq_acc[...] += dot(rows_of(i, pair, h * FW), ds_buf[h, pair], TN)

        for g in range(group):
            col = (h * group + g) * FW
            dq_ref[i, :, col : col + FW] = (dq_acc[:, g * SPAN : (g + 1) * SPAN].T * scale).astype(BF16)

    def term(h, c):
        total = part[h, inv[0, c]]
        for i in range(1, ob):
            total = total + part[i * heads + h, inv[i, c]]
        return total

    def x_copy(h, other):
        return pltpu.make_async_remote_copy(
            src_ref=xsend[h].at[other],
            dst_ref=xrecv[h].at[other],
            send_sem=x_send_sem.at[h, other],
            recv_sem=x_recv_sem.at[h, other],
            device_id=(partner, z),
            device_id_type=MESH,
        )

    def s_copy(h, target, source):
        return pltpu.make_async_remote_copy(
            src_ref=ssend[h].at[target],
            dst_ref=srecv[h].at[source],
            send_sem=s_send_sem.at[h, target],
            recv_sem=s_recv_sem.at[h, source],
            device_id=(2 * target + core, z),
            device_id_type=MESH,
        )

    def for_chips(when, body):
        for other in range(n_chip):
            pl.when(when(other))(functools.partial(body, other))

    def swap_terms(h):
        def fill(other):
            for j in range(ob):
                xsend[h][other, j] = term(h, (2 * other + 1 - core) * ob + j).astype(BF16)

        for_chips(lambda other: other < chip + core, fill)
        for_chips(lambda other: other < chip + core, lambda other: x_copy(h, other).start())

    def send_terms(h):
        def fill(other):
            for j in range(ob):
                total = term(h, (2 * other + core) * ob + j) + xrecv[h][other, j].astype(F32)
                ssend[h][other, j] = total.astype(BF16)

        for_chips(lambda other: other < chip + 1 - core, lambda other: x_copy(h, other).wait_recv())
        for_chips(lambda other: other < chip, fill)
        for_chips(lambda other: other < chip, lambda other: s_copy(h, other, chip).start())

    def own_terms(h):
        for j in range(ob):
            own[h, j] = term(h, me * ob + j)

    def finish_terms(h):
        def add(source):
            own[h] += srecv[h][source].astype(F32)

        for_chips(lambda source: source > chip, lambda source: s_copy(h, chip, source).wait_recv())
        for_chips(lambda source: source > chip, add)

        def add_partner(other):
            own[h] += xrecv[h][other].astype(F32)

        for_chips(lambda other: jnp.logical_and(other == chip, core == 0), add_partner)

        dk_ref[:, :, h * FW : (h + 1) * FW] = own[h, :, :, 0:FW].astype(BF16)
        dv_ref[:, :, h * FW : (h + 1) * FW] = own[h, :, :, FW : 2 * FW].astype(BF16)

    inputs[2].wait()
    project_own(0)
    for d in range(1, n_head - 1):
        hand_on(0, d)
        if d == 1:
            take(0, 1)
            for i in range(1, ob):
                pl.when(outer)(functools.partial(send_own, i))

            @pl.loop(0, chip)
            def _(other):
                copy = kv_copy(2 * other + core, partner, kvf_send.at[other])
                copy.wait_recv()
                copy.start()

            for i in range(1, ob):
                pl.when(inner)(functools.partial(send_own, i))
    project_at(0, 1)
    inputs[4].wait()
    for i in range(ob):
        table(i)

    @pl.loop(0, chip + core)
    def _(other):
        kv_copy(2 * other + 1 - core, partner, kvf_send.at[0]).wait_recv()

    kv_loc[pl.ds(me * ob, ob)] = kv_own[...]

    @pl.loop(0, me)
    def _(owner):
        kv_loc[pl.ds(owner * ob, ob)] = kv_all[owner]

    later = [(i, d) for i in range(1, ob) for d in range(1, n_head - 1)]
    for i in range(ob):
        for h in range(heads):
            softmax(i, h)
            if later:
                hand_on(*later.pop(0))
    for i, d in later:
        hand_on(i, d)
    for d in range(2, n_head):
        take(0, d)
        project_at(0, d)
    finish_projection(0)
    for i in range(1, ob):
        for h in range(heads):
            gradients(i - 1, h)
            query_gradient(i - 1, h)
        project_own(i)
        for d in range(1, n_head):
            take(i, d)
            project_at(i, d)
        finish_projection(i)
    for h in range(heads):
        gradients(ob - 1, h)
        swap_terms(h)
        own_terms(h)
        send_terms(h)
    for h in range(heads):
        query_gradient(ob - 1, h)
    for h in range(heads):
        finish_terms(h)

    for half in range(ob):
        @pl.when(z > 0)
        def _(half=half):
            dy_copy(half, z, dy_ref.at[half], True).wait_send()

            @pl.loop(z + 1, n_head)
            def _(shard):
                dy_copy(half, shard, dy_all.at[shard, half], True).wait_send()

        @pl.when(z < n_head - 1)
        def _(half=half):
            dy_copy(half, z, dy_ref.at[half], False).wait_send()

            @pl.loop(0, z)
            def _(shard):
                dy_copy(half, shard, dy_all.at[shard, half], False).wait_send()

    @pl.when(core == 0)
    def _():
        kv_copy(me, partner, kvf_send.at[chip], kv_own).wait_send()

    @pl.loop(0, chip)
    def _(other):
        kv_copy(2 * other + core, partner, kvf_send.at[other]).wait_send()

    @pl.loop(chip + 1, n_chip)
    def _(other):
        kv_copy(me, 2 * other + core, kv_send.at[other], kv_own).wait_send()

    for h in range(heads):
        for_chips(lambda other: other < chip + core, lambda other: x_copy(h, other).wait_send())
        for_chips(lambda other: other < chip, lambda other: s_copy(h, other, chip).wait_send())


def hand_out(dq, dk, dv, dq_out, dk_out, dv_out):
    dq_out[...] = dq[...]
    dk_out[...] = dk[...]
    dv_out[...] = dv[...]


def per_device(n_ctx, n_head, queries, keys, values, d_y, w_out, key_blocks, block_count):
    tokens, qw = queries.shape
    kvw = keys.shape[1]
    dh = d_y.shape[1]
    ob = tokens // SPAN
    heads = kvw // FW
    group = qw // kvw
    slots = key_blocks.shape[1]
    n_chip = n_ctx // 2
    units = ob * heads
    rows = group * SPAN
    vmem = pl.BlockSpec(memory_space=pltpu.VMEM)
    anywhere = pl.BlockSpec(memory_space=pl.ANY)
    smem = pl.BlockSpec(memory_space=pltpu.SMEM)
    dma = pltpu.SemaphoreType.DMA
    tiles = (n_chip, ob, SPAN, 2 * FW)

    def blocks(a):
        return a.reshape(ob, SPAN, a.shape[1])

    dq, dk, dv = pl.pallas_call(
        functools.partial(kernel, n_ctx, n_head, ob, slots, heads, group),
        out_shape=(
            jax.ShapeDtypeStruct((ob, SPAN, qw), BF16),
            jax.ShapeDtypeStruct((ob, SPAN, kvw), BF16),
            jax.ShapeDtypeStruct((ob, SPAN, kvw), BF16),
        ),
        in_specs=[anywhere, smem, anywhere, anywhere, anywhere, anywhere, anywhere],
        out_specs=(vmem, vmem, vmem),
        scratch_shapes=[
            pltpu.SMEM(key_blocks.shape[::-1], jnp.int32),
            pltpu.VMEM((ob, SPAN, qw), BF16),
            dma((5,)),
            pltpu.VMEM((ob, SPAN, 2 * kvw), BF16),
            pltpu.VMEM((n_ctx, ob, SPAN, 2 * kvw), BF16),
            pltpu.VMEM((n_ctx * ob, SPAN, 2 * kvw), BF16),
            pltpu.VMEM((n_head, ob, SPAN, dh), BF16),
            pltpu.VMEM((n_head, qw, dh), BF16),
            pltpu.SMEM((ob, n_ctx * ob), jnp.int32),
            pltpu.VMEM((units, FW, rows), BF16),
            pltpu.VMEM((units, rows, FW), BF16),
            pltpu.VMEM((units, FW, rows), BF16),
            pltpu.VMEM((units, rows, FW), BF16),
            pltpu.VMEM((qw, SPAN), F32),
            pltpu.VMEM((units, FW, rows), F32),
            pltpu.VMEM((units, -(-slots // PAIR), PAIR * SPAN, rows), F32),
            pltpu.VMEM((FW, rows), F32),
            pltpu.VMEM((units, slots + 1, SPAN, 2 * FW), F32),
            pltpu.VMEM((heads, ob, SPAN, 2 * FW), F32),
            pltpu.VMEM((units, 1, rows), F32),
            pltpu.VMEM((heads, -(-slots // PAIR), PAIR * SPAN, rows), BF16),
            dma((n_head,)),
            dma((ob, n_head)),
            dma((ob, n_head)),
            dma((ob, n_head)),
            dma((n_chip,)),
            dma((n_chip,)),
            dma((n_ctx,)),
            dma((heads, n_chip)),
            dma((heads, n_chip)),
            dma((heads, n_chip)),
            dma((heads, n_chip)),
            *[pltpu.VMEM(tiles, BF16) for _ in range(4 * heads)],
        ],
        compiler_params=pltpu.CompilerParams(
            collective_id=0, has_side_effects=True, vmem_limit_bytes=60 * 1024 * 1024
        ),
        cost_estimate=pl.CostEstimate(
            flops=2 * tokens * dh * n_head * qw, bytes_accessed=2 * w_out.size, transcendentals=0
        ),
    )(key_blocks.T, block_count, blocks(queries), blocks(keys), blocks(values), blocks(d_y), w_out)
    dq, dk, dv = pl.pallas_call(
        hand_out,
        out_shape=tuple(jax.ShapeDtypeStruct(a.shape, a.dtype) for a in (dq, dk, dv)),
        in_specs=[vmem] * 3,
        out_specs=(vmem,) * 3,
        compiler_params=pltpu.CompilerParams(vmem_limit_bytes=60 * 1024 * 1024),
    )(dq, dk, dv)
    return dq.reshape(tokens, qw), dk.reshape(tokens, kvw), dv.reshape(tokens, kvw)


def solution(mesh):
    sharded = P("ctx", "head")
    return jax.shard_map(
        functools.partial(per_device, mesh.shape["ctx"], mesh.shape["head"]),
        mesh=mesh,
        in_specs=(sharded, sharded, sharded, sharded, P("head", None), P(), P()),
        out_specs=(sharded, sharded, sharded),
        check_vma=False,
    )
```

```python
import functools
import math

import jax
import jax.numpy as jnp
from jax import lax
from jax.experimental import pallas as pl
from jax.experimental.pallas import tpu as pltpu
from jax.sharding import PartitionSpec as P

FW = 128
SPAN = 128
PAIR = 2
PIECES = 2
MESH = pl.DeviceIdType.MESH
F32 = jnp.float32
BF16 = jnp.bfloat16


def dot(a, b, dims):
    return lax.dot_general(a, b, (dims, ((), ())), preferred_element_type=F32)


NN = ((1,), (0,))
NT = ((1,), (1,))
TN = ((0,), (0,))


def kernel(
    n_ctx, n_head, ob, slots, heads, group,
    kb_hbm, cnt_ref, q_hbm, k_hbm, v_hbm, dy_ref, w_ref,
    dq_ref, dk_ref, dv_ref,
    kb_ref, q_ref, in_sem,
    kv_own, kv_all, kv_loc, dy_all, w_buf, inv, qt, qn, gt, gn, gacc, ot, p_buf, dq_acc, part, own, share, ds_buf,
    w_sem, dn_send, up_send, dy_recv, kv_send, kvf_send, kv_recv, x_send_sem, x_recv_sem, s_send_sem, s_recv_sem, *exchange,
):
    scale = 1.0 / math.sqrt(FW)
    me = lax.axis_index("ctx")
    z = lax.axis_index("head")
    core = lax.rem(me, 2)
    chip = me // 2
    partner = me + 1 - 2 * core
    n_chip = n_ctx // 2
    kvw = heads * FW
    rows = group * SPAN
    xsend, xrecv, ssend, srecv = (exchange[e * heads : (e + 1) * heads] for e in range(4))

    barrier = pltpu.get_barrier_semaphore()

    @pl.loop(1, n_ctx)
    def _(step):
        pl.semaphore_signal(
            barrier, inc=1, device_id=(lax.rem(me + step, n_ctx), z), device_id_type=MESH
        )

    @pl.when(z > 0)
    def _():
        pl.semaphore_signal(barrier, inc=1, device_id=(me, z - 1), device_id_type=MESH)

    @pl.when(z < n_head - 1)
    def _():
        pl.semaphore_signal(barrier, inc=1, device_id=(me, z + 1), device_id_type=MESH)

    dh = dy_ref.shape[2]

    def w_copy(shard):
        return pltpu.make_async_copy(
            w_ref.at[:, pl.ds(pl.multiple_of(shard * dh, dh), dh)], w_buf.at[shard], w_sem.at[shard]
        )

    inputs = [
        pltpu.make_async_copy(src, dst, in_sem.at[e])
        for e, (src, dst) in enumerate(
            [
                (k_hbm, kv_own.at[:, :, 0:kvw]),
                (v_hbm, kv_own.at[:, :, kvw : 2 * kvw]),
                (dy_ref, dy_all.at[z]),
                (q_hbm, q_ref),
                (kb_hbm, kb_ref),
            ]
        )
    ]
    for copy in inputs:
        copy.start()

    @pl.loop(0, n_head)
    def _(step):
        w_copy(lax.rem(z + step, n_head)).start()

    ends = jnp.where(z > 0, 1, 0) + jnp.where(z < n_head - 1, 1, 0)
    pl.semaphore_wait(barrier, n_ctx - 1 + ends)

    part_rows = SPAN // PIECES

    def dy_copy(half, shard, src, down):
        sems = dn_send if down else up_send
        return [
            pltpu.make_async_remote_copy(
                src_ref=src.at[piece * part_rows : (piece + 1) * part_rows],
                dst_ref=dy_all.at[shard, half, piece * part_rows : (piece + 1) * part_rows],
                send_sem=sems.at[half, shard, piece],
                recv_sem=dy_recv.at[half, shard, piece],
                device_id=(me, z - 1 if down else z + 1),
                device_id_type=MESH,
            )
            for piece in range(PIECES)
        ]

    def send_own(half):
        @pl.when(z > 0)
        def _():
            for copy in dy_copy(half, z, dy_ref.at[half], True):
                copy.start()

        @pl.when(z < n_head - 1)
        def _():
            for copy in dy_copy(half, z, dy_ref.at[half], False):
                copy.start()

    inner = jnp.logical_and(z > 0, z < n_head - 1)
    outer = jnp.logical_not(inner)

    def hand_on(half, d):
        @pl.when(jnp.logical_and(inner, z + d < n_head))
        def _():
            for copy in dy_copy(half, z + d, dy_all.at[z + d, half], True):
                copy.wait_recv()
                copy.start()

        @pl.when(jnp.logical_and(inner, z - d >= 0))
        def _():
            for copy in dy_copy(half, z - d, dy_all.at[z - d, half], False):
                copy.wait_recv()
                copy.start()

    def take(half, d):
        @pl.when(jnp.logical_and(outer, z + d < n_head))
        def _():
            for copy in dy_copy(half, z + d, dy_all.at[z + d, half], True):
                copy.wait_recv()

        @pl.when(jnp.logical_and(outer, z - d >= 0))
        def _():
            for copy in dy_copy(half, z - d, dy_all.at[z - d, half], False):
                copy.wait_recv()

    send_own(0)
    inputs[0].wait()
    inputs[1].wait()

    def kv_copy(owner, target, sem, src=None):
        return pltpu.make_async_remote_copy(
            src_ref=kv_all.at[owner] if src is None else src,
            dst_ref=kv_all.at[owner],
            send_sem=sem,
            recv_sem=kv_recv.at[owner],
            device_id=(target, z),
            device_id_type=MESH,
        )

    @pl.when(core == 0)
    def _():
        kv_copy(me, partner, kvf_send.at[chip], kv_own).start()

    @pl.loop(chip + 1, n_chip)
    def _(other):
        kv_copy(me, 2 * other + core, kv_send.at[other], kv_own).start()

    def table(i):
        blk = me * ob + i
        count = cnt_ref[blk]

        @pl.loop(0, (me + 1) * ob)
        def _(c):
            def look(s, found):
                hit = jnp.logical_and(kb_ref[s, blk] == c, s < count)
                return jnp.where(hit, s, found)

            inv[i, c] = lax.fori_loop(0, slots, look, jnp.int32(slots))

    inputs[3].wait()
    for i in range(ob):
        for h in range(heads):
            u = i * heads + h
            part[u, slots] = jnp.zeros((SPAN, 2 * FW), F32)
            for g in range(group):
                col = (h * group + g) * FW
                tile = q_ref[i, :, col : col + FW]
                qn[u, g * SPAN : (g + 1) * SPAN, :] = tile
                qt[u, :, g * SPAN : (g + 1) * SPAN] = tile.astype(F32).T.astype(BF16)

    def project(half, shard, dy):
        if half == 0:
            w_copy(shard).wait()
        gacc[...] += dot(w_buf[shard], dy, NT)

    def project_at(half, d):
        @pl.when(z + d < n_head)
        def _():
            project(half, z + d, dy_all[z + d, half])

        @pl.when(z - d >= 0)
        def _():
            project(half, z - d, dy_all[z - d, half])

    def project_own(half):
        gacc[...] = jnp.zeros_like(gacc)
        project(half, z, dy_all[z, half])

    def finish_projection(half):
        for h in range(heads):
            u = half * heads + h
            for g in range(group):
                row = (h * group + g) * FW
                tile = gacc[row : row + FW, :]
                gt[u, :, g * SPAN : (g + 1) * SPAN] = tile.astype(BF16)
                gn[u, g * SPAN : (g + 1) * SPAN, :] = tile.T.astype(BF16)

    def block_of(i, slot):
        blk = me * ob + i
        live = slot < cnt_ref[blk]
        c = jnp.where(live, kb_ref[slot, blk], blk)
        return c, jnp.where(live, (blk - c) * SPAN, -4 * SPAN)

    def rows_of(i, pair, col):
        return jnp.concatenate(
            [kv_loc[block_of(i, pair * PAIR + e)[0], :, col : col + FW] for e in range(PAIR)], axis=0
        )

    def pairs(i):
        return (jnp.minimum((me * ob + i) // 2 + 1, slots) + PAIR - 1) // PAIR

    def softmax(i, h):
        u = i * heads + h
        ahead = lax.broadcasted_iota(jnp.int32, (SPAN, rows), 0) - lax.rem(
            lax.broadcasted_iota(jnp.int32, (SPAN, rows), 1), SPAN
        )

        def scores(pair, top):
            s = dot(rows_of(i, pair, h * FW), qt[u], NN)
            masked = [
                jnp.where(ahead <= block_of(i, pair * PAIR + e)[1], s[e * SPAN : (e + 1) * SPAN], -1e30)
                for e in range(PAIR)
            ]
            s = jnp.concatenate(masked, axis=0)
            p_buf[u, pair] = s
            return jnp.maximum(top, jnp.max(s, axis=0, keepdims=True))

        top = lax.fori_loop(0, pairs(i), scores, jnp.full((1, rows), -1e30, F32))

        ot[u] = jnp.zeros((FW, rows), F32)

        def exps(pair, total):
            e = jnp.exp((p_buf[u, pair] - top) * scale)
            p_buf[u, pair] = e
            high = e.astype(BF16)
            low = (e - high.astype(F32)).astype(BF16)
            v = rows_of(i, pair, kvw + h * FW)
            ot[u] += dot(v, high, TN) + dot(v, low, TN)
            return total + jnp.sum(e, axis=0, keepdims=True)

        total = lax.fori_loop(0, pairs(i), exps, jnp.zeros((1, rows), F32))
        share[u] = 1.0 / total

    def gradients(i, h):
        u = i * heads + h
        part_of = share[u]
        delta = jnp.sum(gt[u].astype(F32) * ot[u], axis=0, keepdims=True) * part_of

        @pl.loop(0, pairs(i))
        def _(pair):
            p = p_buf[u, pair] * part_of
            dp = dot(rows_of(i, pair, kvw + h * FW), gt[u], NN)
            ds = (p * (dp - delta)).astype(BF16)
            dk = dot(ds, qn[u], NN) * scale
            dv = dot(p.astype(BF16), gn[u], NN)
            both = jnp.concatenate([dk, dv], axis=1)
            for e in range(PAIR):
                part[u, pair * PAIR + e] = both[e * SPAN : (e + 1) * SPAN]
            ds_buf[h, pair] = ds

    def query_gradient(i, h):
        dq_acc[...] = jnp.zeros_like(dq_acc)

        @pl.loop(0, pairs(i))
        def _(pair):
            dq_acc[...] += dot(rows_of(i, pair, h * FW), ds_buf[h, pair], TN)

        for g in range(group):
            col = (h * group + g) * FW
            dq_ref[i, :, col : col + FW] = (dq_acc[:, g * SPAN : (g + 1) * SPAN].T * scale).astype(BF16)

    def term(h, c):
        total = part[h, inv[0, c]]
        for i in range(1, ob):
            total = total + part[i * heads + h, inv[i, c]]
        return total

    def x_copy(h, other):
        return pltpu.make_async_remote_copy(
            src_ref=xsend[h].at[other],
            dst_ref=xrecv[h].at[other],
            send_sem=x_send_sem.at[h, other],
            recv_sem=x_recv_sem.at[h, other],
            device_id=(partner, z),
            device_id_type=MESH,
        )

    def s_copy(h, target, source):
        return pltpu.make_async_remote_copy(
            src_ref=ssend[h].at[target],
            dst_ref=srecv[h].at[source],
            send_sem=s_send_sem.at[h, target],
            recv_sem=s_recv_sem.at[h, source],
            device_id=(2 * target + core, z),
            device_id_type=MESH,
        )

    def for_chips(when, body):
        for other in range(n_chip):
            pl.when(when(other))(functools.partial(body, other))

    def swap_terms(h):
        def fill(other):
            for j in range(ob):
                xsend[h][other, j] = term(h, (2 * other + 1 - core) * ob + j).astype(BF16)

        for_chips(lambda other: other < chip + core, fill)
        for_chips(lambda other: other < chip + core, lambda other: x_copy(h, other).start())

    def send_terms(h):
        def fill(other):
            for j in range(ob):
                total = term(h, (2 * other + core) * ob + j) + xrecv[h][other, j].astype(F32)
                ssend[h][other, j] = total.astype(BF16)

        for_chips(lambda other: other < chip + 1 - core, lambda other: x_copy(h, other).wait_recv())
        for_chips(lambda other: other < chip, fill)
        for_chips(lambda other: other < chip, lambda other: s_copy(h, other, chip).start())

    def own_terms(h):
        for j in range(ob):
            own[h, j] = term(h, me * ob + j)

    def finish_terms(h):
        def add(source):
            own[h] += srecv[h][source].astype(F32)

        for_chips(lambda source: source > chip, lambda source: s_copy(h, chip, source).wait_recv())
        for_chips(lambda source: source > chip, add)

        def add_partner(other):
            own[h] += xrecv[h][other].astype(F32)

        for_chips(lambda other: jnp.logical_and(other == chip, core == 0), add_partner)

        dk_ref[:, :, h * FW : (h + 1) * FW] = own[h, :, :, 0:FW].astype(BF16)
        dv_ref[:, :, h * FW : (h + 1) * FW] = own[h, :, :, FW : 2 * FW].astype(BF16)

    inputs[2].wait()
    project_own(0)
    for d in range(1, n_head - 1):
        hand_on(0, d)
        if d == 1:
            take(0, 1)
            for i in range(1, ob):
                pl.when(outer)(functools.partial(send_own, i))

            @pl.loop(0, chip)
            def _(other):
                copy = kv_copy(2 * other + core, partner, kvf_send.at[other])
                copy.wait_recv()
                copy.start()

            for i in range(1, ob):
                pl.when(inner)(functools.partial(send_own, i))
    project_at(0, 1)
    inputs[4].wait()
    for i in range(ob):
        table(i)

    @pl.loop(0, chip + core)
    def _(other):
        kv_copy(2 * other + 1 - core, partner, kvf_send.at[0]).wait_recv()

    kv_loc[pl.ds(me * ob, ob)] = kv_own[...]

    @pl.loop(0, me)
    def _(owner):
        kv_loc[pl.ds(owner * ob, ob)] = kv_all[owner]

    later = [(i, d) for i in range(1, ob) for d in range(1, n_head - 1)]
    for i in range(ob):
        for h in range(heads):
            softmax(i, h)
            if later:
                hand_on(*later.pop(0))
    for i, d in later:
        hand_on(i, d)
    for d in range(2, n_head):
        take(0, d)
        project_at(0, d)
    finish_projection(0)
    for i in range(1, ob):
        for h in range(heads):
            gradients(i - 1, h)
            query_gradient(i - 1, h)
        project_own(i)
        for d in range(1, n_head):
            take(i, d)
            project_at(i, d)
        finish_projection(i)
    for h in range(heads):
        gradients(ob - 1, h)
        swap_terms(h)
        own_terms(h)
        send_terms(h)
    for h in range(heads):
        query_gradient(ob - 1, h)
    for h in range(heads):
        finish_terms(h)

    for half in range(ob):
        @pl.when(z > 0)
        def _(half=half):
            for copy in dy_copy(half, z, dy_ref.at[half], True):
                copy.wait_send()

            @pl.loop(z + 1, n_head)
            def _(shard):
                for copy in dy_copy(half, shard, dy_all.at[shard, half], True):
                    copy.wait_send()

        @pl.when(z < n_head - 1)
        def _(half=half):
            for copy in dy_copy(half, z, dy_ref.at[half], False):
                copy.wait_send()

            @pl.loop(0, z)
            def _(shard):
                for copy in dy_copy(half, shard, dy_all.at[shard, half], False):
                    copy.wait_send()

    @pl.when(core == 0)
    def _():
        kv_copy(me, partner, kvf_send.at[chip], kv_own).wait_send()

    @pl.loop(0, chip)
    def _(other):
        kv_copy(2 * other + core, partner, kvf_send.at[other]).wait_send()

    @pl.loop(chip + 1, n_chip)
    def _(other):
        kv_copy(me, 2 * other + core, kv_send.at[other], kv_own).wait_send()

    for h in range(heads):
        for_chips(lambda other: other < chip + core, lambda other: x_copy(h, other).wait_send())
        for_chips(lambda other: other < chip, lambda other: s_copy(h, other, chip).wait_send())


def hand_out(dq, dk, dv, dq_out, dk_out, dv_out):
    dq_out[...] = dq[...]
    dk_out[...] = dk[...]
    dv_out[...] = dv[...]


def per_device(n_ctx, n_head, queries, keys, values, d_y, w_out, key_blocks, block_count):
    tokens, qw = queries.shape
    kvw = keys.shape[1]
    dh = d_y.shape[1]
    ob = tokens // SPAN
    heads = kvw // FW
    group = qw // kvw
    slots = key_blocks.shape[1]
    n_chip = n_ctx // 2
    units = ob * heads
    rows = group * SPAN
    vmem = pl.BlockSpec(memory_space=pltpu.VMEM)
    anywhere = pl.BlockSpec(memory_space=pl.ANY)
    smem = pl.BlockSpec(memory_space=pltpu.SMEM)
    dma = pltpu.SemaphoreType.DMA
    tiles = (n_chip, ob, SPAN, 2 * FW)

    def blocks(a):
        return a.reshape(ob, SPAN, a.shape[1])

    dq, dk, dv = pl.pallas_call(
        functools.partial(kernel, n_ctx, n_head, ob, slots, heads, group),
        out_shape=(
            jax.ShapeDtypeStruct((ob, SPAN, qw), BF16),
            jax.ShapeDtypeStruct((ob, SPAN, kvw), BF16),
            jax.ShapeDtypeStruct((ob, SPAN, kvw), BF16),
        ),
        in_specs=[anywhere, smem, anywhere, anywhere, anywhere, anywhere, anywhere],
        out_specs=(vmem, vmem, vmem),
        scratch_shapes=[
            pltpu.SMEM(key_blocks.shape[::-1], jnp.int32),
            pltpu.VMEM((ob, SPAN, qw), BF16),
            dma((5,)),
            pltpu.VMEM((ob, SPAN, 2 * kvw), BF16),
            pltpu.VMEM((n_ctx, ob, SPAN, 2 * kvw), BF16),
            pltpu.VMEM((n_ctx * ob, SPAN, 2 * kvw), BF16),
            pltpu.VMEM((n_head, ob, SPAN, dh), BF16),
            pltpu.VMEM((n_head, qw, dh), BF16),
            pltpu.SMEM((ob, n_ctx * ob), jnp.int32),
            pltpu.VMEM((units, FW, rows), BF16),
            pltpu.VMEM((units, rows, FW), BF16),
            pltpu.VMEM((units, FW, rows), BF16),
            pltpu.VMEM((units, rows, FW), BF16),
            pltpu.VMEM((qw, SPAN), F32),
            pltpu.VMEM((units, FW, rows), F32),
            pltpu.VMEM((units, -(-slots // PAIR), PAIR * SPAN, rows), F32),
            pltpu.VMEM((FW, rows), F32),
            pltpu.VMEM((units, slots + 1, SPAN, 2 * FW), F32),
            pltpu.VMEM((heads, ob, SPAN, 2 * FW), F32),
            pltpu.VMEM((units, 1, rows), F32),
            pltpu.VMEM((heads, -(-slots // PAIR), PAIR * SPAN, rows), BF16),
            dma((n_head,)),
            dma((ob, n_head, PIECES)),
            dma((ob, n_head, PIECES)),
            dma((ob, n_head, PIECES)),
            dma((n_chip,)),
            dma((n_chip,)),
            dma((n_ctx,)),
            dma((heads, n_chip)),
            dma((heads, n_chip)),
            dma((heads, n_chip)),
            dma((heads, n_chip)),
            *[pltpu.VMEM(tiles, BF16) for _ in range(4 * heads)],
        ],
        compiler_params=pltpu.CompilerParams(
            collective_id=0, has_side_effects=True, vmem_limit_bytes=60 * 1024 * 1024
        ),
        cost_estimate=pl.CostEstimate(
            flops=2 * tokens * dh * n_head * qw, bytes_accessed=2 * w_out.size, transcendentals=0
        ),
    )(key_blocks.T, block_count, blocks(queries), blocks(keys), blocks(values), blocks(d_y), w_out)
    dq, dk, dv = pl.pallas_call(
        hand_out,
        out_shape=tuple(jax.ShapeDtypeStruct(a.shape, a.dtype) for a in (dq, dk, dv)),
        in_specs=[vmem] * 3,
        out_specs=(vmem,) * 3,
        compiler_params=pltpu.CompilerParams(vmem_limit_bytes=60 * 1024 * 1024),
    )(dq, dk, dv)
    return dq.reshape(tokens, qw), dk.reshape(tokens, kvw), dv.reshape(tokens, kvw)


def solution(mesh):
    sharded = P("ctx", "head")
    return jax.shard_map(
        functools.partial(per_device, mesh.shape["ctx"], mesh.shape["head"]),
        mesh=mesh,
        in_specs=(sharded, sharded, sharded, sharded, P("head", None), P(), P()),
        out_specs=(sharded, sharded, sharded),
        check_vma=False,
    )
```
